32 devices in a mesh: group: 2 (over core), replica: 16 (over z, y, x).
Axes of the slice: x: 2, y: 2, z: 4, core: 2. Of those that a mesh axis runs over, the one named last changes fastest.
Arguments:
- latents: bfloat16 [16, 1024, 1024], P('replica', 'group'), may hold values from -6 to 6
- cond: bfloat16 [16, 1024], P('replica'), may hold values from -6 to 6
- cotangent: bfloat16 [16, 1024, 1024], P('replica', 'group'), may hold values from -6 to 6
- ada_weight: bfloat16 [1024, 6144], P('group'), may hold values from -0.1875 to 0.1875
- ada_bias: bfloat16 [6144], P('group'), may hold values from -4 to 4
- qkv_weight: bfloat16 [1024, 3072], P('group'), may hold values from -0.1875 to 0.1875
- query_bias: bfloat16 [1024], P('group'), may hold values from -4 to 4
- value_bias: bfloat16 [1024], P('group'), may hold values from -4 to 4
- output_weight: bfloat16 [1024, 1024], P('group'), may hold values from -0.75 to 0.75
- output_bias: bfloat16 [1024], P('group'), may hold values from -4 to 4
- up_weight: bfloat16 [1024, 4096], P('group'), may hold values from -0.1875 to 0.1875
- up_bias: bfloat16 [4096], P('group'), may hold values from -4 to 4
- down_weight: bfloat16 [4096, 1024], P('group'), may hold values from -0.09375 to 0.09375
- down_bias: bfloat16 [1024], P('group'), may hold values from -4 to 4
Outputs:
- block_out: bfloat16 [16, 1024, 1024], P('replica', 'group')
- latents_grad: float32 [16, 1024, 1024], P('replica', 'group')
- cond_grad: float32 [16, 1024], P('replica')
- ada_weight_grad: float32 [1024, 6144], P('group')
- ada_bias_grad: float32 [6144], P('group')
- qkv_weight_grad: float32 [1024, 3072], P('group')
- query_bias_grad: float32 [1024], P('group')
- value_bias_grad: float32 [1024], P('group')
- output_weight_grad: float32 [1024, 1024], P('group')
- output_bias_grad: float32 [1024], P('group')
- up_weight_grad: float32 [1024, 4096], P('group')
- up_bias_grad: float32 [4096], P('group')
- down_weight_grad: float32 [4096, 1024], P('group')
- down_bias_grad: float32 [1024], P('group')
The draws below stay inside these ranges and needn't reach their ends.
All inputs are finite; a program needn't handle non-finite values.
Results may differ from the reference program's by a relative error of at most 0.02.
The reference program's roundings to bfloat16 on the way (of `silu_cond`, `attn_in`, `mixed`, `mlp_in` and `active`) count: a program that leaves them out, or rounds other values in their place, can miss the bound.
Values may be sent and summed in bfloat16 or wider, within the bound.
A program may use at most 256 MiB of HBM per device.

```python
import jax
import jax.numpy as jnp
from jax import lax

D = 1024
HEADS = 16
FF = 4096
SEQ = 1024
LAT_ALL = 16


def levels(own_key, shape, pieces, smallest, largest):
    loudness, own = 1.0, jax.random.fold_in(own_key, 6)
    for axis_at, shards_of in pieces:
        steps = jnp.exp(jax.random.uniform(jax.random.fold_in(own, axis_at), (shards_of,), jnp.float32, smallest / len(pieces), largest / len(pieces)))
        loudness = loudness * jnp.repeat(steps, shape[axis_at] // shards_of).reshape([-1 if axis == axis_at else 1 for axis in range(len(shape))])
    return loudness


def centred(own_key, dims, scale, limit, cuts=(), dtype=jnp.bfloat16):
    result = jax.random.normal(own_key, dims, jnp.float32) * scale
    if len(cuts) > 0:
        result = levels(own_key, dims, cuts, -0.22, 0.18) * result
    return jnp.clip(result, min=-limit, max=limit).astype(dtype)


def setup_inputs(seed: int = 0) -> dict:
    seeds = jax.random.split(jax.random.key(seed), 15)
    return {
        "latents": centred(seeds[0], (LAT_ALL, SEQ, D), 1.0, 6.0, ((0, 16), (1, 2))),
        "cond": centred(seeds[1], (LAT_ALL, D), 1.0, 6.0, ((0, 16),)),
        "cotangent": centred(seeds[2], (LAT_ALL, SEQ, D), 1.0, 6.0, ((0, 16), (1, 2))),
        "ada_weight": centred(seeds[3], (D, 6 * D), D ** -0.5, 0.1875, ((0, 2),)),
        "ada_bias": centred(seeds[4], (6 * D,), 0.3, 4.0, ((0, 2),)),
        "qkv_weight": centred(seeds[5], (D, 3 * D), D ** -0.5, 0.1875, ((0, 2),)),
        "query_bias": centred(seeds[6], (D,), 0.3, 4.0, ((0, 2),)),
        "value_bias": centred(seeds[7], (D,), 0.3, 4.0, ((0, 2),)),
        "output_weight": centred(seeds[8], (D, D), (D // 16) ** -0.5, 0.75, ((0, 2),)),
        "output_bias": centred(seeds[9], (D,), 0.3, 4.0, ((0, 2),)),
        "up_weight": centred(seeds[10], (D, FF), D ** -0.5, 0.1875, ((0, 2),)),
        "up_bias": centred(seeds[11], (FF,), 0.3, 4.0, ((0, 2),)),
        "down_weight": centred(seeds[12], (FF, D), FF ** -0.5, 0.09375, ((0, 2),)),
        "down_bias": centred(seeds[13], (D,), 0.3, 4.0, ((0, 2),)),
    }


@jax.custom_vjp
def low(v):
    return lax.optimization_barrier(v.astype(jnp.bfloat16)).astype(jnp.float32)

@jax.custom_vjp
def low_back(v):
    return v

def low_keep(v):
    return (low(v), None)

def low_pass(kept, grad):
    return (grad,)

def back_keep(v):
    return (v, None)

def back_low(kept, grad):
    return (low(grad),)
low.defvjp(low_keep, low_pass)
low_back.defvjp(back_keep, back_low)

def matmul(left, right):
    return jnp.dot(left, right, precision=lax.Precision.HIGHEST)

def layer_norm(values):
    center = values - lax.optimization_barrier(jnp.mean(values, axis=-1, keepdims=True))
    spread = lax.optimization_barrier(jnp.mean(center * center, axis=-1, keepdims=True))
    return center * lax.rsqrt(spread + 1e-06)

def one_latent(params, latent_in, modulation):
    qkv_weight, query_bias, value_bias, output_weight, output_bias, up_weight, up_bias, down_weight, down_bias = params
    length = latent_in.shape[0]
    width = latent_in.shape[1]
    head_dim = width // HEADS
    factor = head_dim ** (-0.5)
    parts = [modulation[index * width:(index + 1) * width] for index in range(6)]
    shift_one, scale_one, gate_one, shift_two, scale_two, gate_two = parts
    normed_one = layer_norm(latent_in)
    attn_in = low(normed_one * (1.0 + scale_one) + shift_one)
    projected = matmul(attn_in, qkv_weight)
    queries = low_back(low(projected[:, :width] + query_bias))
    key_rows = low_back(low(projected[:, width:2 * width]))
    value_rows = low_back(low(projected[:, 2 * width:] + value_bias))
    query_heads = queries.reshape(length, HEADS, head_dim)
    key_heads = key_rows.reshape(length, HEADS, head_dim)
    value_heads = value_rows.reshape(length, HEADS, head_dim)
    scores = low_back(jnp.einsum('qhd,khd->hqk', query_heads, key_heads, precision=lax.Precision.HIGHEST) * factor)
    top_score = lax.optimization_barrier(jnp.max(scores, axis=-1, keepdims=True))
    expo = jnp.exp(scores - top_score)
    weights_soft = expo / lax.optimization_barrier(jnp.sum(expo, axis=-1, keepdims=True))
    mixed = jnp.einsum('hqk,khd->qhd', low(weights_soft), value_heads, precision=lax.Precision.HIGHEST)
    mixed = low_back(low(mixed.reshape(length, width)))
    branch_one = low_back(matmul(mixed, output_weight)) + output_bias
    middle = latent_in + gate_one * branch_one
    normed_two = layer_norm(middle)
    mlp_in = low(normed_two * (1.0 + scale_two) + shift_two)
    hidden = low_back(matmul(mlp_in, up_weight)) + up_bias
    active = low_back(low(jax.nn.gelu(hidden, approximate=True)))
    branch_two = low_back(matmul(active, down_weight)) + down_bias
    return middle + gate_two * branch_two

def forward_all(latents, cond, ada_weight, ada_bias, *params):
    silu_cond = low(jax.nn.silu(cond))
    modulation = low_back(matmul(silu_cond, ada_weight)) + ada_bias
    step = jax.checkpoint(lambda pair: one_latent(params, pair[0], pair[1]))
    return lax.map(step, (latents, modulation))

def reference(latents, cond, cotangent, ada_weight, ada_bias, qkv_weight, query_bias, value_bias, output_weight, output_bias, up_weight, up_bias, down_weight, down_bias):
    inputs = (latents, cond, ada_weight, ada_bias, qkv_weight, query_bias, value_bias, output_weight, output_bias, up_weight, up_bias, down_weight, down_bias)
    floats = tuple((item.astype(jnp.float32) for item in inputs))
    block_out, back_fn = jax.vjp(forward_all, *floats)
    grads = back_fn(cotangent.astype(jnp.float32))
    return (block_out.astype(jnp.bfloat16), grads[0], grads[1], grads[2], grads[3], grads[4], grads[5], grads[6], grads[7], grads[8], grads[9], grads[10], grads[11], grads[12])
```

```python
import functools

import jax
import jax.numpy as jnp
from jax import lax
from jax.experimental import pallas as pl
from jax.experimental.pallas import tpu as pltpu
from jax.sharding import PartitionSpec as P

HEADS = 16


def norm_rows(values):
    center = values - jnp.mean(values, axis=-1, keepdims=True)
    inverse = lax.rsqrt(jnp.mean(center * center, axis=-1, keepdims=True) + 1e-06)
    return (center * inverse, inverse)


def norm_back(normed, inverse, grad_normed):
    first = jnp.mean(grad_normed, axis=-1, keepdims=True)
    second = jnp.mean(grad_normed * normed, axis=-1, keepdims=True)
    return inverse * (grad_normed - first - normed * second)


def token_sum(values):
    return jnp.sum(values, axis=1)


def head_masks(width, head_dim, dtype):
    lane = lax.broadcasted_iota(jnp.int32, (1, width), 1)
    return [
        jnp.where((lane >= first) & (lane < first + head_dim), 1.0, 0.0).astype(dtype)
        for first in range(0, width, head_dim)
    ]


def contract(left, right, left_dim, right_dim):
    return lax.dot_general(
        left,
        right,
        (((left_dim,), (right_dim,)), ((), ())),
        preferred_element_type=jnp.float32,
    )


def attend_kernel(head_dim, query_ref, key_ref, value_ref, mixed_ref):
    factor = head_dim ** (-0.5)
    key_part, value_part = key_ref[...], value_ref[...]
    masks = head_masks(key_part.shape[1], head_dim, jnp.bfloat16)
    total_mixed = None
    for mask in masks:
        query_part = query_ref[...] * (mask * factor).astype(jnp.bfloat16)
        scores = contract(query_part, key_part, 1, 1)
        expo = jnp.exp(scores - jnp.max(scores, axis=-1, keepdims=True))
        share = 1.0 / jnp.sum(expo, axis=-1, keepdims=True)
        weights_soft = (expo * share).astype(jnp.bfloat16)
        mixed = contract(weights_soft, value_part * mask, 1, 0)
        total_mixed = mixed if total_mixed is None else total_mixed + mixed
    mixed_ref[...] = total_mixed.astype(mixed_ref.dtype)


def attend_back_kernel(
    head_dim, query_ref, key_ref, value_ref, grad_ref, query_grad_ref, key_grad_ref, value_grad_ref
):
    factor = head_dim ** (-0.5)
    key_part, value_part = key_ref[...], value_ref[...]
    masks = head_masks(key_part.shape[1], head_dim, jnp.bfloat16)
    query_grad = key_grad = value_grad = 0.0
    for mask in masks:
        query_part = query_ref[...] * (mask * factor).astype(jnp.bfloat16)
        grad_part = grad_ref[...] * mask
        scores = contract(key_part, query_part, 1, 1)
        expo = jnp.exp(scores - jnp.max(scores, axis=0, keepdims=True))
        weights_soft = expo * (1.0 / jnp.sum(expo, axis=0, keepdims=True))
        grad_soft = contract(value_part, grad_part, 1, 1)
        inner = jnp.sum(grad_soft * weights_soft, axis=0, keepdims=True)
        grad_scores = (weights_soft * (grad_soft - inner)).astype(jnp.bfloat16)
        value_grad += contract(weights_soft.astype(jnp.bfloat16), grad_part, 1, 0)
        key_grad += contract(grad_scores, query_part, 1, 0)
        query_grad += contract(key_part * mask, grad_scores, 0, 0)
    query_grad_ref[...] = (jnp.transpose(query_grad) * factor).astype(query_grad_ref.dtype)
    key_grad_ref[...] = key_grad
    value_grad_ref[...] = value_grad


def attention(queries, keys, values, head_dim):
    rows, width = queries.shape
    length = keys.shape[0]
    block = max(128, head_dim)
    short = pl.BlockSpec((rows, block), lambda index: (0, index))
    tall = pl.BlockSpec((length, block), lambda index: (0, index))
    return pl.pallas_call(
        functools.partial(attend_kernel, head_dim),
        grid=(width // block,),
        in_specs=[short, tall, tall],
        out_specs=short,
        out_shape=jax.ShapeDtypeStruct((rows, width), jnp.bfloat16),
        compiler_params=pltpu.CompilerParams(vmem_limit_bytes=48 * 2**20),
        cost_estimate=pl.CostEstimate(
            flops=16 * rows * length * width,
            bytes_accessed=4 * (rows + length) * width,
            transcendentals=rows * length * (width // head_dim),
        ),
        name="attend",
    )(queries, keys, values)


def attention_back(queries, keys, values, grads, head_dim):
    rows, width = queries.shape
    length = keys.shape[0]
    block = max(128, head_dim)
    short = pl.BlockSpec((rows, block), lambda index: (0, index))
    tall = pl.BlockSpec((length, block), lambda index: (0, index))
    return pl.pallas_call(
        functools.partial(attend_back_kernel, head_dim),
        grid=(width // block,),
        in_specs=[short, tall, tall, short],
        out_specs=[short, tall, tall],
        out_shape=[
            jax.ShapeDtypeStruct((rows, width), jnp.bfloat16),
            jax.ShapeDtypeStruct((length, width), jnp.float32),
            jax.ShapeDtypeStruct((length, width), jnp.float32),
        ],
        compiler_params=pltpu.CompilerParams(vmem_limit_bytes=48 * 2**20),
        cost_estimate=pl.CostEstimate(
            flops=40 * rows * length * width,
            bytes_accessed=8 * (rows + 2 * length) * width,
            transcendentals=rows * length * (width // head_dim),
        ),
        name="attend_back",
    )(queries, keys, values, grads)


def turn(values, axis, shift):
    count = lax.axis_size(axis)
    return lax.ppermute(values, axis, [(at, (at + shift) % count) for at in range(count)])


def group_rows(left, right, rows):
    count, place = lax.axis_size("group"), lax.axis_index("group")

    def term(owner):
        part = lax.dynamic_slice_in_dim(left, owner * rows, rows, 1)
        return jnp.dot(part.T, right, preferred_element_type=jnp.float32)

    away = [
        turn(term((place + shift) % count).astype(jnp.bfloat16), "group", shift)
        for shift in range(1, count)
    ]
    total = term(place)
    for item in away:
        total = total + item.astype(jnp.float32)
    return total.astype(jnp.bfloat16)


def pair_sum(values, bits):
    place = lax.axis_index("replica")
    pairs = [[(at, at ^ bit) for at in range(lax.axis_size("replica"))] for bit in bits]
    for bit, pair in zip(bits, pairs):
        half = values.shape[0] // 2
        upper = (place & bit) != 0
        low, high = values[:half], values[half:]
        away = lax.ppermute(jnp.where(upper, low, high), "replica", pair)
        values = jnp.where(upper, high, low) + away
    for bit, pair in reversed(list(zip(bits, pairs))):
        upper = (place & bit) != 0
        away = lax.ppermute(values, "replica", pair)
        values = jnp.where(
            upper, jnp.concatenate([away, values]), jnp.concatenate([values, away])
        )
    return values


def replica_sum(values):
    count, rows = lax.axis_size("replica"), values.shape[0]
    if count & (count - 1) or rows % count:
        return lax.psum(values, "replica")
    bits = [1 << step for step in range(count.bit_length() - 1)]
    cut = (values.shape[1] // 256) * 128
    first = pair_sum(values[:, :cut], bits)
    second = pair_sum(values[:, cut:], bits[1:2] + bits[:1] + bits[2:])
    return jnp.concatenate([first, second], axis=1)


def after(values, earlier):
    return lax.optimization_barrier((values, earlier))[0]


def per_device(
    latents,
    cond,
    cotangent,
    ada_weight,
    ada_bias,
    qkv_weight,
    query_bias,
    value_bias,
    output_weight,
    output_bias,
    up_weight,
    up_bias,
    down_weight,
    down_bias,
):
    count_lat, local_len, width = latents.shape
    row_count = count_lat * local_len
    head_dim = width // HEADS
    my_index = lax.axis_index("group")
    gathered = (
        lax.all_gather(qkv_weight, "group", axis=0, tiled=True),
        lax.all_gather(output_weight, "group", axis=0, tiled=True),
        lax.all_gather(up_weight, "group", axis=0, tiled=True),
        lax.all_gather(down_weight, "group", axis=0, tiled=True),
        lax.all_gather(query_bias, "group", axis=0, tiled=True),
        lax.all_gather(value_bias, "group", axis=0, tiled=True),
        lax.all_gather(output_bias, "group", axis=0, tiled=True),
        lax.all_gather(up_bias, "group", axis=0, tiled=True),
        lax.all_gather(down_bias, "group", axis=0, tiled=True),
        lax.all_gather(ada_bias, "group", axis=0, tiled=True),
    )
    (
        qkv_full,
        output_full,
        up_full,
        down_full,
        query_full,
        value_full,
        outbias_full,
        upbias_full,
        downbias_full,
        adabias_full,
    ) = gathered
    cond_float = cond.astype(jnp.float32)
    silu_cond, silu_back = jax.vjp(jax.nn.silu, cond_float)
    silu_low = silu_cond.astype(jnp.bfloat16)
    shard_rows = ada_weight.shape[0]
    silu_mine = lax.dynamic_slice_in_dim(silu_low, my_index * shard_rows, shard_rows, 1)
    partial_mod = jnp.dot(silu_mine, ada_weight, preferred_element_type=jnp.float32)
    modulation = lax.psum(partial_mod, "group") + adabias_full.astype(jnp.float32)
    parts = [modulation[:, None, index * width : (index + 1) * width] for index in range(6)]
    shift_one, scale_one, gate_one, shift_two, scale_two, gate_two = parts
    latent_float = latents.astype(jnp.float32)
    normed_one, inverse_one = norm_rows(latent_float)
    attn_in = (normed_one * (1.0 + scale_one) + shift_one).astype(jnp.bfloat16)
    attn_flat = attn_in.reshape(row_count, width)
    projected = jnp.dot(attn_flat, qkv_full, preferred_element_type=jnp.float32)
    queries = (
        (projected[:, :width] + query_full.astype(jnp.float32))
        .astype(jnp.bfloat16)
        .reshape(count_lat, local_len, width)
    )
    key_rows = (
        projected[:, width : 2 * width].astype(jnp.bfloat16).reshape(count_lat, local_len, width)
    )
    value_rows = (
        (projected[:, 2 * width :] + value_full.astype(jnp.float32))
        .astype(jnp.bfloat16)
        .reshape(count_lat, local_len, width)
    )
    group_count = lax.axis_size("group")
    both = jnp.concatenate([key_rows, value_rows], axis=2)
    both_whole = jnp.concatenate(
        [both] + [turn(both, "group", shift) for shift in range(1, group_count)], axis=1
    )
    key_whole, value_whole = both_whole[:, :, :width], both_whole[:, :, width:]
    mixed_low = jnp.concatenate(
        [
            attention(queries[index], key_whole[index], value_whole[index], head_dim)
            for index in range(count_lat)
        ],
        axis=0,
    )
    branch_one = (
        jnp.dot(mixed_low, output_full, preferred_element_type=jnp.float32)
        + outbias_full.astype(jnp.float32)
    ).reshape(count_lat, local_len, width)
    middle = latent_float + gate_one * branch_one
    normed_two, inverse_two = norm_rows(middle)
    mlp_in = (
        (normed_two * (1.0 + scale_two) + shift_two).astype(jnp.bfloat16).reshape(row_count, width)
    )
    hidden = jnp.dot(mlp_in, up_full, preferred_element_type=jnp.float32) + upbias_full.astype(
        jnp.float32
    )
    active, gelu_back = jax.vjp(lambda values: jax.nn.gelu(values, approximate=True), hidden)
    active_low = active.astype(jnp.bfloat16)
    branch_two = (
        jnp.dot(active_low, down_full, preferred_element_type=jnp.float32)
        + downbias_full.astype(jnp.float32)
    ).reshape(count_lat, local_len, width)
    block_out = (middle + gate_two * branch_two).astype(jnp.bfloat16)
    grad_out = cotangent.astype(jnp.float32)
    grad_gate_two = token_sum(grad_out * branch_two)
    grad_branch_two = (grad_out * gate_two).reshape(row_count, width)
    down_bias_term = jnp.sum(grad_branch_two, axis=0)
    branch_two_low = grad_branch_two.astype(jnp.bfloat16)
    down_share = group_rows(active_low, branch_two_low, down_weight.shape[0])
    grad_active = jnp.dot(branch_two_low, down_full.T, preferred_element_type=jnp.float32).astype(
        jnp.bfloat16
    )
    grad_hidden = gelu_back(grad_active.astype(jnp.float32))[0]
    up_bias_term = jnp.sum(grad_hidden, axis=0)
    hidden_low = grad_hidden.astype(jnp.bfloat16)
    up_share = group_rows(mlp_in, hidden_low, up_weight.shape[0])
    down_sum, up_sum = lax.psum((down_share, up_share), "replica")
    grad_mlp_in = jnp.dot(hidden_low, up_full.T, preferred_element_type=jnp.float32).reshape(
        count_lat, local_len, width
    )
    grad_shift_two = token_sum(grad_mlp_in)
    grad_scale_two = token_sum(grad_mlp_in * normed_two)
    grad_middle = grad_out + norm_back(normed_two, inverse_two, grad_mlp_in * (1.0 + scale_two))
    grad_gate_one = token_sum(grad_middle * branch_one)
    grad_branch_one = (grad_middle * gate_one).reshape(row_count, width)
    output_bias_term = jnp.sum(grad_branch_one, axis=0)
    branch_one_low = grad_branch_one.astype(jnp.bfloat16)
    output_share = group_rows(mixed_low, branch_one_low, output_weight.shape[0])
    grad_mixed = (
        jnp.dot(branch_one_low, output_full.T, preferred_element_type=jnp.float32)
        .astype(jnp.bfloat16)
        .reshape(count_lat, local_len, width)
    )

    grad_mixed = after(grad_mixed, up_share)
    pieces = [
        attention_back(
            queries[index], key_whole[index], value_whole[index], grad_mixed[index], head_dim
        )
        for index in range(count_lat)
    ]
    grad_query, key_terms, value_terms = [jnp.stack(items) for items in zip(*pieces)]
    grad_key, grad_value = key_terms[:, :local_len], value_terms[:, :local_len]
    for shift in range(1, group_count):
        block = slice(shift * local_len, (shift + 1) * local_len)
        grad_key = grad_key + turn(key_terms[:, block], "group", -shift)
        grad_value = grad_value + turn(value_terms[:, block], "group", -shift)
    query_low = grad_query.astype(jnp.bfloat16).reshape(row_count, width)
    key_low = grad_key.astype(jnp.bfloat16).reshape(row_count, width)
    value_low = grad_value.astype(jnp.bfloat16).reshape(row_count, width)
    query_bias_term = jnp.sum(query_low.astype(jnp.float32), axis=0)
    value_bias_term = jnp.sum(value_low.astype(jnp.float32), axis=0)
    grad_qkv = jnp.concatenate([query_low, key_low, value_low], axis=1)
    qkv_share = group_rows(attn_flat, grad_qkv, qkv_weight.shape[0])
    late_sum = replica_sum(jnp.concatenate([output_share, qkv_share], axis=1))
    output_sum, qkv_sum = late_sum[:, :width], late_sum[:, width:]
    grad_attn_in = jnp.dot(grad_qkv, qkv_full.T, preferred_element_type=jnp.float32).reshape(
        count_lat, local_len, width
    )
    grad_shift_one = token_sum(grad_attn_in)
    grad_scale_one = token_sum(grad_attn_in * normed_one)
    latents_grad = grad_middle + norm_back(
        normed_one, inverse_one, grad_attn_in * (1.0 + scale_one)
    )
    mod_terms = jnp.concatenate(
        [
            grad_shift_one,
            grad_scale_one,
            grad_gate_one,
            grad_shift_two,
            grad_scale_two,
            grad_gate_two,
        ],
        axis=1,
    )
    bias_terms = (
        query_bias_term,
        value_bias_term,
        output_bias_term,
        up_bias_term,
        down_bias_term,
    )
    bias_rows_all = jnp.concatenate(
        [term.reshape(group_count, -1) for term in bias_terms], axis=1
    )
    bias_share = lax.psum_scatter(bias_rows_all, "group", scatter_dimension=0, tiled=True)
    share_len = bias_share.shape[1]
    bias_spread = jnp.concatenate(
        [bias_share, jnp.zeros((count_lat - 1, share_len), jnp.float32)], axis=0
    )
    small = jnp.concatenate([mod_terms, silu_mine.astype(jnp.float32), bias_spread], axis=1)
    every = lax.all_gather(small, ("replica", "group"), axis=0).reshape(
        -1, group_count, count_lat, small.shape[1]
    )
    mod_every = jnp.sum(every[..., : 6 * width], axis=1).reshape(-1, 6 * width)
    mine_every = lax.dynamic_index_in_dim(every, my_index, 1, keepdims=False)
    mine_every = mine_every[..., 6 * width :].reshape(-1, shard_rows + share_len)
    silu_every = mine_every[:, :shard_rows].astype(jnp.bfloat16)
    bias_sum = jnp.sum(mine_every[:, shard_rows:], axis=0)
    grad_mod_low = mod_every.astype(jnp.bfloat16)
    bias_rows = ada_bias.shape[0]
    ada_bias_grad = lax.dynamic_slice_in_dim(
        jnp.sum(mod_every, axis=0), my_index * bias_rows, bias_rows, 0
    )
    ada_weight_grad = jnp.dot(silu_every.T, grad_mod_low, preferred_element_type=jnp.float32)
    grad_mod_mine = lax.dynamic_slice_in_dim(
        grad_mod_low, lax.axis_index("replica") * count_lat, count_lat, 0
    )
    silu_piece = jnp.dot(grad_mod_mine, ada_weight.T, preferred_element_type=jnp.float32)
    silu_grad = lax.all_gather(silu_piece, "group", axis=1, tiled=True)
    cond_grad = silu_back(silu_grad)[0]
    cuts, at = [], 0
    for term in bias_terms:
        cuts.append(bias_sum[at : at + term.shape[0] // group_count])
        at += term.shape[0] // group_count
    query_bias_grad, value_bias_grad, output_bias_grad, up_bias_grad, down_bias_grad = cuts
    return (
        block_out,
        latents_grad,
        cond_grad,
        ada_weight_grad,
        ada_bias_grad,
        qkv_sum.astype(jnp.float32),
        query_bias_grad,
        value_bias_grad,
        output_sum.astype(jnp.float32),
        output_bias_grad,
        up_sum.astype(jnp.float32),
        up_bias_grad,
        down_sum.astype(jnp.float32),
        down_bias_grad,
    )


def solution(mesh):
    return jax.shard_map(
        per_device,
        mesh=mesh,
        in_specs=(
            P("replica", "group", None),
            P("replica", None),
            P("replica", "group", None),
            P("group", None),
            P("group"),
            P("group", None),
            P("group"),
            P("group"),
            P("group", None),
            P("group"),
            P("group", None),
            P("group"),
            P("group", None),
            P("group"),
        ),
        out_specs=(
            P("replica", "group", None),
            P("replica", "group", None),
            P("replica", None),
            P("group", None),
            P("group"),
            P("group", None),
            P("group"),
            P("group"),
            P("group", None),
            P("group"),
            P("group", None),
            P("group"),
            P("group", None),
            P("group"),
        ),
        check_vma=False,
    )
```
